32 devices in a mesh: rows: 8 (over z, x), rhs: 4 (over y, core).
Axes of the slice: x: 2, y: 2, z: 4, core: 2. Of those that a mesh axis runs over, the one named last changes fastest.
Arguments:
- start: bfloat16 [128, 16384], P('rhs', 'rows')
- tiles: bfloat16 [128, 12, 128, 128], P('rows'), may hold values from -0.21875 to 0.21875
- cols: int32 [128, 12], P('rows'), may hold values from 0 to 127, as said below
- counts: int32 [128], P('rows'), may hold values from 3 to 12
Outputs:
- basis: bfloat16 [4, 128, 16384], P(None, 'rhs', 'rows')
- gram: float32 [4, 160, 160], P('rhs')
The draws below stay inside these ranges and needn't reach their ends.
Inputs may be any that keep to these rules, and one draw needn't show every extreme that they name: cols[b, t] names a row block held by the same index of rows as b or by the index on either side of it: b // 16 - 1 <= cols[b, t] // 16 <= b // 16 + 1.
All inputs are finite; a program needn't handle non-finite values.
Results may differ from the reference program's by a relative error of at most 0.015.
Values sent between devices are 32-bit elements; how exact they have to be, the bound alone decides.
A program may use at most 64 MiB of HBM per device.

```python
import jax
import jax.numpy as jnp
from jax import lax

BLK = 128
PANEL = 32
S = 4
NT = 12
RB = 16
NBLK = 128
NROWS = 16384
RHS = 128
N_ROWS = 8
N_RHS = 4


def draw_start(key, part):
    key = jax.random.fold_in(key, 11)
    rising = 1.0 + 2.0 * jnp.arange(NROWS, dtype=jnp.float32) / NROWS
    values = jnp.clip(jax.random.normal(key, (RHS, NROWS), jnp.float32), -6.0, 6.0) * rising[None, :]
    return values.astype(jnp.bfloat16)


def draw_cols(key, part):
    key = jax.random.fold_in(key, 12)
    owner = jnp.arange(NBLK, dtype=jnp.int32) // RB
    offset = jax.random.randint(key, (NBLK, NT), -RB, 2 * RB, dtype=jnp.int32)
    column = jnp.clip(owner[:, None] * RB + offset, 0, NBLK - 1)
    column = column.at[0, 0].set(0).at[NBLK - 1, 0].set(NBLK - 1)
    return column.astype(jnp.int32)


def draw_counts(key, part):
    key = jax.random.fold_in(key, 13)
    first_key, second_key, third_key, fourth_key = jax.random.split(key, 4)
    device_ids = jnp.arange(N_ROWS, dtype=jnp.int32)
    heavy_device = (jax.random.randint(first_key, (N_ROWS,), 0, 8, dtype=jnp.int32) == 0) & (device_ids > 0)
    heavy_block = jnp.repeat(heavy_device, RB)
    light = jax.random.randint(second_key, (NBLK,), NT // 4, NT // 2 + 1, dtype=jnp.int32)
    result = jnp.where(heavy_block, NT, light)
    top_place = jax.random.randint(third_key, (N_ROWS,), 0, RB, dtype=jnp.int32)
    step_away = jax.random.randint(fourth_key, (N_ROWS,), 1, RB, dtype=jnp.int32)
    low_place = (top_place + step_away) % RB
    position = jnp.arange(NBLK, dtype=jnp.int32) % RB
    result = jnp.where(position == jnp.repeat(top_place, RB), NT, result)
    low_here = (position == jnp.repeat(low_place, RB)) & jnp.logical_not(heavy_block)
    result = jnp.where(low_here, NT // 4, result)
    return result.astype(jnp.int32)


def levels(key, dims, cuts, least, largest):
    level = 1.0
    for dim, blocks in cuts:
        draws = jax.random.uniform(jax.random.fold_in(jax.random.fold_in(key, 6), dim), (blocks,), jnp.float32, least / len(cuts), largest / len(cuts))
        level = level * jnp.repeat(jnp.exp(draws), dims[dim] // blocks).reshape((-1,) + (1,) * (len(dims) - 1 - dim))
    return level


def noise(stream_key, dims, scale, limit, cuts=(), held_as=jnp.bfloat16):
    factor_of = levels(stream_key, dims, cuts, -0.22, 0.18) if cuts else 1.0
    values = jax.random.normal(stream_key, dims, jnp.float32) * scale * factor_of
    return jnp.minimum(jnp.maximum(values, -limit), limit).astype(held_as)


def setup_inputs(seed: int = 0) -> dict:
    splits = jax.random.split(jax.random.key(seed), 5)
    start = draw_start(jax.random.fold_in(splits[4], 71), 0)
    tiles = noise(splits[1], (NBLK, NT, BLK, BLK), (BLK * NT // 2) ** -0.5, 0.21875, ((0, 8),))
    cols = draw_cols(jax.random.fold_in(splits[4], 71), 0)
    counts = draw_counts(jax.random.fold_in(splits[4], 71), 0)
    return dict(start=start, tiles=tiles, cols=cols, counts=counts)


def apply_transposed(vector, tiles, cols, live):
    rhs_count = vector.shape[0]
    block_count = cols.shape[0]
    blocked = vector.reshape(rhs_count, block_count, BLK)
    groups = block_count // RB

    def one_group(group, total):
        low = (group * RB).astype(jnp.int32)
        xpart = lax.dynamic_slice_in_dim(blocked, low, RB, 1).astype(jnp.float32)
        tpart = lax.dynamic_slice_in_dim(tiles, low, RB, 0).astype(jnp.float32)
        cpart = lax.dynamic_slice_in_dim(cols, low, RB, 0)
        lpart = lax.dynamic_slice_in_dim(live, low, RB, 0)
        contrib = jnp.einsum("pri,rtij->rtpj", xpart, tpart, precision=lax.Precision.HIGHEST)
        contrib = contrib * lpart[:, :, None, None]
        contrib = contrib.reshape(RB * NT, rhs_count, BLK).transpose(1, 0, 2)
        return total.at[:, cpart.reshape(-1), :].add(contrib)

    total = jnp.zeros((rhs_count, block_count, BLK), jnp.float32)
    total = lax.fori_loop(0, groups, one_group, total)
    return total.reshape(rhs_count, block_count * BLK).astype(jnp.bfloat16)


def reference(start, tiles, cols, counts):
    live = (jnp.arange(NT, dtype=jnp.int32)[None, :] < counts[:, None]).astype(jnp.float32)
    vector = start
    powers = []
    for power in range(S):
        vector = apply_transposed(vector, tiles, cols, live)
        powers.append(vector)
    basis = jnp.stack(powers)
    everything = jnp.concatenate([start[None], basis], axis=0)
    total_rows = everything.shape[2]
    grams = []
    for panel_index in range(N_RHS):
        stacked = everything[:, panel_index * PANEL:(panel_index + 1) * PANEL, :]
        stacked = stacked.reshape((S + 1) * PANEL, total_rows)
        product = lax.dot_general(stacked, stacked, (((1,), (1,)), ((), ())), preferred_element_type=jnp.float32)
        grams.append(product / total_rows)
    return basis, jnp.stack(grams)
```

```python
import functools

import jax
import jax.numpy as jnp
from jax import lax
from jax.experimental import pallas as pl
from jax.experimental.pallas import tpu as pltpu
from jax.sharding import PartitionSpec as P

S = 4
HALVES = 2
CHUNKS = 2
UNROLL = 16
MESH = pl.DeviceIdType.MESH


def schedule(cols, counts, devices):
    blocks, slots = cols.shape
    total = blocks * slots
    r = lax.axis_index("rows")
    rel = cols - (r - 1) * blocks
    side = rel // blocks
    even = r % 2 == 0
    group = jnp.where(side == 1, 2, jnp.where((side == 0) == even, 0, 1))
    target = group * blocks + rel % blocks
    used = jnp.arange(slots, dtype=jnp.int32)[None, :] < counts[:, None]
    target = jnp.where(used, target, 3 * blocks).reshape(-1)
    item = jnp.arange(total, dtype=jnp.int32)
    earlier = target[None, :] < target[:, None]
    tied = (target[None, :] == target[:, None]) & (item[None, :] < item[:, None])
    rank = jnp.sum(earlier | tied, axis=1, dtype=jnp.int32)
    opens = jnp.logical_not(jnp.any(tied, axis=1)).astype(jnp.int32)
    code = ((item // slots) * total + item) * 2 + opens
    placed = jnp.sum(jnp.where(rank[None, :] == item[:, None], code[None, :], 0), axis=1, dtype=jnp.int32)
    c = jnp.arange(3 * blocks, dtype=jnp.int32)[:, None]
    upto = jnp.sum(target[None, :] <= c, axis=1, dtype=jnp.int32)
    here = jnp.any(target[None, :] == c, axis=1)
    last = jnp.where(here, upto - 1, total)
    return jnp.concatenate([placed, last])


def kernel(
    n, blocks, slots, start_ref, tiles_hbm, code_ref, basis_ref, gram_ref,
    tiles, x, sums0, sums1, far_out, far_in, near_out, near_in,
    early, early_in, late, late_in,
    tile_sem, far_send, far_recv, near_send, near_recv, gram_send, gram_recv,
):
    total = blocks * slots
    sums = (sums0, sums1)
    rows = start_ref.shape[0] // HALVES
    blk = tiles.shape[-1]
    per = blocks // CHUNKS
    stages = n.bit_length() - 1
    r = lax.axis_index("rows")
    parity = r % 2
    step = 4 * parity - 2
    to, frm = r + step, r - step
    sends_far = jnp.logical_and(to >= 0, to < n)
    takes_far = jnp.logical_and(frm >= 0, frm < n)
    to = jnp.clip(to, 0, n - 1)
    frm = jnp.clip(frm, 0, n - 1)
    partner = r + 1 - 2 * parity

    def across(stage):
        width = 1 << stage
        return r + width - 2 * width * ((r // width) % 2)

    load = pltpu.make_async_copy(tiles_hbm, tiles, tile_sem)
    load.start()

    barrier = pltpu.get_barrier_semaphore()
    for stage in range(stages):
        pl.semaphore_signal(barrier, inc=1, device_id={"rows": across(stage)}, device_id_type=MESH)

    @pl.when(sends_far)
    def _():
        pl.semaphore_signal(barrier, inc=1, device_id={"rows": to}, device_id_type=MESH)

    @pl.when(takes_far)
    def _():
        pl.semaphore_signal(barrier, inc=1, device_id={"rows": frm}, device_id_type=MESH)

    for h in range(HALVES):
        sums[h][total] = jnp.zeros((rows, blk), jnp.float32)
        for b in range(blocks):
            x[h, b] = start_ref[h * rows : (h + 1) * rows, b * blk : (b + 1) * blk]
    pl.semaphore_wait(barrier, stages + sends_far.astype(jnp.int32) + takes_far.astype(jnp.int32))
    load.wait()

    def far_copy(k, h, j):
        part = pl.ds(j * per, per)
        return pltpu.make_async_remote_copy(
            src_ref=far_out.at[k, h, part], dst_ref=far_in.at[k, h, part],
            send_sem=far_send.at[k, h, j], recv_sem=far_recv.at[k, h, j],
            device_id={"rows": to}, device_id_type=MESH,
        )

    def near_copy(k, h, j):
        part = pl.ds(j * per, per)
        return pltpu.make_async_remote_copy(
            src_ref=near_out.at[k, h, part], dst_ref=near_in.at[k, h, part],
            send_sem=near_send.at[k, h, j], recv_sem=near_recv.at[k, h, j],
            device_id={"rows": partner}, device_id_type=MESH,
        )

    def gram_copy(which, stage):
        src, dst = (early, early_in) if which == 0 else (late, late_in)
        return pltpu.make_async_remote_copy(
            src_ref=src.at[stage], dst_ref=dst.at[stage],
            send_sem=gram_send.at[which, stage], recv_sem=gram_recv.at[which, stage],
            device_id={"rows": across(stage)}, device_id_type=MESH,
        )

    def compute(k, h):
        place = sums[h]

        def some(i, acc):
            for u in range(UNROLL):
                s = i * UNROLL + u
                code = code_ref[s]
                opens = code & 1
                both = code >> 1
                b = both // total
                product = jnp.dot(
                    x[h, b], tiles[both - b * total], preferred_element_type=jnp.float32
                )
                acc = jnp.where(opens == 1, 0.0, acc) + product
                place[s] = acc
            return acc

        lax.fori_loop(0, total // UNROLL, some, jnp.zeros((rows, blk), jnp.float32))
        for j in range(CHUNKS):
            for c in range(j * per, (j + 1) * per):
                far_out[k, h, c] = place[code_ref[total + c]]

            @pl.when(sends_far)
            def _():
                far_copy(k, h, j).start()

    def relay(k, h):
        place = sums[h]
        for j in range(CHUNKS):
            for c in range(j * per, (j + 1) * per):
                near_out[k, h, c] = place[code_ref[total + blocks + c]]

            @pl.when(takes_far)
            def _():
                far_copy(k, h, j).wait_recv()
                part = pl.ds(j * per, per)
                near_out[k, h, part] += far_in[k, h, part]

            near_copy(k, h, j).start()

    def finish(k, h):
        place = sums[h]
        for j in range(CHUNKS):
            near_copy(k, h, j).wait_recv()
            for c in range(j * per, (j + 1) * per):
                value = (place[code_ref[total + 2 * blocks + c]] + near_in[k, h, c]).astype(jnp.bfloat16)
                x[h, c] = value
                basis_ref[k, h * rows : (h + 1) * rows, c * blk : (c + 1) * blk] = value

    NT = (((1,), (1,)), ((), ()))
    cut = 2 * blk

    def strips(lo, hi, columns):
        parts = [start_ref[:, columns]] if lo == 0 else []
        parts += [basis_ref[k, :, columns] for k in range(max(lo - 1, 0), hi - 1)]
        return parts[0] if len(parts) == 1 else jnp.concatenate(parts, axis=0)

    def early_gram():
        acc = None
        for i in range(blocks * blk // cut):
            w = strips(0, S, slice(i * cut, (i + 1) * cut))
            d = lax.dot_general(w, w, NT, preferred_element_type=jnp.float32)
            acc = d if acc is None else acc + d
        early[0] = acc

    def late_gram():
        panel = HALVES * rows
        acc, own = None, None
        for i in range(blocks * blk // cut):
            columns = slice(i * cut, (i + 1) * cut)
            w = strips(0, S, columns)
            v = strips(S, S + 1, columns)
            d = lax.dot_general(v, w, NT, preferred_element_type=jnp.float32)
            e = lax.dot_general(v, v, NT, preferred_element_type=jnp.float32)
            acc = d if acc is None else acc + d
            own = e if own is None else own + e
        late[0, 0:panel, :] = acc
        late[0, panel : 2 * panel, :] = jnp.zeros_like(acc)
        late[0, panel : 2 * panel, 0:panel] = own

    def join(which, stage):
        src, dst = (early, early_in) if which == 0 else (late, late_in)
        gram_copy(which, stage).wait_recv()
        src[stage + 1] = src[stage] + dst[stage]
        if stage + 1 < stages:
            gram_copy(which, stage + 1).start()

    pending = []
    for k in range(S):
        for h in range(HALVES):
            if k > 0:
                finish(k - 1, h)
            compute(k, h)
        if k == S - 1:
            early_gram()
            gram_copy(0, 0).start()
        for h in range(HALVES):
            relay(k, h)
            if k == S - 1 and h < stages:
                join(0, h)
    for h in range(HALVES):
        finish(S - 1, h)
    late_gram()
    gram_copy(1, 0).start()
    for stage in range(stages):
        if stage >= HALVES:
            join(0, stage)
        join(1, stage)

    panel = HALVES * rows
    scale = 1.0 / (n * blocks * blk)
    w = S * panel
    gram_ref[0, 0:w, 0:w] = early[stages] * scale
    side = late[stages, 0:panel, :] * scale
    gram_ref[0, w : w + panel, 0:w] = side
    gram_ref[0, 0:w, w : w + panel] = side.T
    gram_ref[0, w : w + panel, w : w + panel] = late[stages, panel : 2 * panel, 0:panel] * scale

    for k in range(S):
        for h in range(HALVES):
            for j in range(CHUNKS):
                near_copy(k, h, j).wait_send()

                @pl.when(sends_far)
                def _():
                    far_copy(k, h, j).wait_send()

    for which in range(2):
        for stage in range(stages):
            gram_copy(which, stage).wait_send()


def body(n, start, tiles, cols, counts):
    panel, rows_dev = start.shape
    blocks, slots, blk, _ = tiles.shape
    total = blocks * slots
    rows = panel // HALVES
    stages = n.bit_length() - 1
    code = schedule(cols, counts, n)
    w = S * panel
    vmem = pl.BlockSpec(memory_space=pltpu.VMEM)
    travel = pltpu.VMEM((S, HALVES, blocks, rows, blk), jnp.float32)
    dma = pltpu.SemaphoreType.DMA
    return pl.pallas_call(
        functools.partial(kernel, n, blocks, slots),
        out_shape=(
            jax.ShapeDtypeStruct((S, panel, rows_dev), jnp.bfloat16),
            jax.ShapeDtypeStruct((1, w + panel, w + panel), jnp.float32),
        ),
        in_specs=[vmem, pl.BlockSpec(memory_space=pl.ANY), pl.BlockSpec(memory_space=pltpu.SMEM)],
        out_specs=(vmem, vmem),
        scratch_shapes=[
            pltpu.VMEM((total, blk, blk), jnp.bfloat16),
            pltpu.VMEM((HALVES, blocks, rows, blk), jnp.bfloat16),
            pltpu.VMEM((total + 1, rows, blk), jnp.float32),
            pltpu.VMEM((total + 1, rows, blk), jnp.float32),
            travel, travel, travel, travel,
            pltpu.VMEM((stages + 1, w, w), jnp.float32),
            pltpu.VMEM((stages, w, w), jnp.float32),
            pltpu.VMEM((stages + 1, 2 * panel, w), jnp.float32),
            pltpu.VMEM((stages, 2 * panel, w), jnp.float32),
            dma,
            dma((S, HALVES, CHUNKS)),
            dma((S, HALVES, CHUNKS)),
            dma((S, HALVES, CHUNKS)),
            dma((S, HALVES, CHUNKS)),
            dma((2, stages)),
            dma((2, stages)),
        ],
        compiler_params=pltpu.CompilerParams(
            collective_id=0, has_side_effects=True, vmem_limit_bytes=40 * 1024 * 1024
        ),
    )(start, tiles.reshape(total, blk, blk), code)


def solution(mesh):
    return jax.shard_map(
        functools.partial(body, mesh.shape["rows"]),
        mesh=mesh,
        in_specs=(P("rhs", "rows"), P("rows", None, None, None), P("rows", None), P("rows")),
        out_specs=(P(None, "rhs", "rows"), P("rhs", None, None)),
        check_vma=False,
    )
```

```python
import functools

import jax
import jax.numpy as jnp
from jax import lax
from jax.experimental import pallas as pl
from jax.experimental.pallas import tpu as pltpu
from jax.sharding import PartitionSpec as P

S = 4
HALVES = 2
CHUNKS = 4
UNROLL = 16
MESH = pl.DeviceIdType.MESH


def schedule(cols, counts, devices):
    blocks, slots = cols.shape
    total = blocks * slots
    r = lax.axis_index("rows")
    rel = cols - (r - 1) * blocks
    side = rel // blocks
    even = r % 2 == 0
    group = jnp.where(side == 1, 2, jnp.where((side == 0) == even, 0, 1))
    target = group * blocks + rel % blocks
    used = jnp.arange(slots, dtype=jnp.int32)[None, :] < counts[:, None]
    target = jnp.where(used, target, 3 * blocks).reshape(-1)
    item = jnp.arange(total, dtype=jnp.int32)
    earlier = target[None, :] < target[:, None]
    tied = (target[None, :] == target[:, None]) & (item[None, :] < item[:, None])
    rank = jnp.sum(earlier | tied, axis=1, dtype=jnp.int32)
    opens = jnp.logical_not(jnp.any(tied, axis=1)).astype(jnp.int32)
    code = item * 2 + opens
    placed = jnp.sum(jnp.where(rank[None, :] == item[:, None], code[None, :], 0), axis=1, dtype=jnp.int32)
    c = jnp.arange(3 * blocks, dtype=jnp.int32)[:, None]
    upto = jnp.sum(target[None, :] <= c, axis=1, dtype=jnp.int32)
    here = jnp.any(target[None, :] == c, axis=1)
    last = jnp.where(here, upto - 1, total)
    return jnp.concatenate([placed, last])


def kernel(
    n, blocks, slots, start_ref, tiles, code_ref, basis_ref, gram_ref,
    products, sums0, sums1, far_out, far_in, near_out, near_in,
    gram0, gram0_in, gram1, gram1_in, gram2, gram2_in,
    far_send, far_recv, near_send, near_recv, gram_send, gram_recv,
):
    total = blocks * slots
    sums = (sums0, sums1)
    grams = ((gram0, gram0_in), (gram1, gram1_in), (gram2, gram2_in))
    rows = start_ref.shape[0] // HALVES
    blk = tiles.shape[-1]
    per = blocks // CHUNKS
    stages = n.bit_length() - 1
    r = lax.axis_index("rows")
    parity = r % 2
    step = 4 * parity - 2
    to, frm = r + step, r - step
    sends_far = jnp.logical_and(to >= 0, to < n)
    takes_far = jnp.logical_and(frm >= 0, frm < n)
    to = jnp.clip(to, 0, n - 1)
    frm = jnp.clip(frm, 0, n - 1)
    partner = r + 1 - 2 * parity

    def across(stage):
        width = 1 << stage
        return r + width - 2 * width * ((r // width) % 2)

    barrier = pltpu.get_barrier_semaphore()
    for stage in range(stages):
        pl.semaphore_signal(barrier, inc=1, device_id={"rows": across(stage)}, device_id_type=MESH)

    @pl.when(sends_far)
    def _():
        pl.semaphore_signal(barrier, inc=1, device_id={"rows": to}, device_id_type=MESH)

    @pl.when(takes_far)
    def _():
        pl.semaphore_signal(barrier, inc=1, device_id={"rows": frm}, device_id_type=MESH)

    for h in range(HALVES):
        sums[h][total] = jnp.zeros((rows, blk), jnp.float32)
    pl.semaphore_wait(barrier, stages + sends_far.astype(jnp.int32) + takes_far.astype(jnp.int32))

    def far_copy(k, h, j):
        part = pl.ds(j * per, per)
        return pltpu.make_async_remote_copy(
            src_ref=far_out.at[k, h, part], dst_ref=far_in.at[k, h, part],
            send_sem=far_send.at[k, h, j], recv_sem=far_recv.at[k, h, j],
            device_id={"rows": to}, device_id_type=MESH,
        )

    def near_copy(k, h, j):
        part = pl.ds(j * per, per)
        return pltpu.make_async_remote_copy(
            src_ref=near_out.at[k, h, part], dst_ref=near_in.at[k, h, part],
            send_sem=near_send.at[k, h, j], recv_sem=near_recv.at[k, h, j],
            device_id={"rows": partner}, device_id_type=MESH,
        )

    def gram_copy(which, stage):
        src, dst = grams[which]
        return pltpu.make_async_remote_copy(
            src_ref=src.at[stage], dst_ref=dst.at[stage],
            send_sem=gram_send.at[which, stage], recv_sem=gram_recv.at[which, stage],
            device_id={"rows": across(stage)}, device_id_type=MESH,
        )

    zero = jnp.zeros((rows, blk), jnp.bfloat16)

    def multiply(pair, upper, lower):
        a, b = 2 * pair * slots, (2 * pair + 1) * slots
        left = jnp.concatenate(
            [jnp.concatenate([upper, zero], axis=1), jnp.concatenate([zero, lower], axis=1)], axis=0
        )
        for t in range(0, slots, 2):
            right = jnp.concatenate(
                [
                    jnp.concatenate([tiles[a + t], tiles[a + t + 1]], axis=1),
                    jnp.concatenate([tiles[b + t], tiles[b + t + 1]], axis=1),
                ],
                axis=0,
            )
            out = jnp.dot(left, right, preferred_element_type=jnp.float32)
            products[a + t] = out[:rows, :blk]
            products[a + t + 1] = out[:rows, blk:]
            products[b + t] = out[rows:, :blk]
            products[b + t + 1] = out[rows:, blk:]

    def advance(k, h):
        for j in range(CHUNKS):
            if k > 0:
                values = finish(k - 1, h, j)
            else:
                values = [
                    start_ref[h * rows : (h + 1) * rows, c * blk : (c + 1) * blk]
                    for c in range(j * per, (j + 1) * per)
                ]
            for p in range(per // 2):
                multiply(j * per // 2 + p, values[2 * p], values[2 * p + 1])

    def collect(k, h):
        place = sums[h]

        def some(i, acc):
            for u in range(UNROLL):
                s = i * UNROLL + u
                code = code_ref[s]
                acc = jnp.where((code & 1) == 1, 0.0, acc) + products[code >> 1]
                place[s] = acc
            return acc

        lax.fori_loop(0, total // UNROLL, some, jnp.zeros((rows, blk), jnp.float32))
        for j in range(CHUNKS):
            for c in range(j * per, (j + 1) * per):
                far_out[k, h, c] = place[code_ref[total + c]]

            @pl.when(sends_far)
            def _():
                far_copy(k, h, j).start()

    def relay(k, h):
        place = sums[h]
        for j in range(CHUNKS):
            for c in range(j * per, (j + 1) * per):
                near_out[k, h, c] = place[code_ref[total + blocks + c]]

            @pl.when(takes_far)
            def _():
                far_copy(k, h, j).wait_recv()
                part = pl.ds(j * per, per)
                near_out[k, h, part] += far_in[k, h, part]

            near_copy(k, h, j).start()

    def finish(k, h, j):
        place = sums[h]
        near_copy(k, h, j).wait_recv()
        values = []
        for c in range(j * per, (j + 1) * per):
            value = (place[code_ref[total + 2 * blocks + c]] + near_in[k, h, c]).astype(jnp.bfloat16)
            basis_ref[k, h * rows : (h + 1) * rows, c * blk : (c + 1) * blk] = value
            values.append(value)
        return values

    NT = (((1,), (1,)), ((), ()))
    panel = HALVES * rows
    cut = 2 * blk

    def strips(lo, hi, columns):
        parts = [start_ref[:, columns]] if lo == 0 else []
        parts += [basis_ref[k, :, columns] for k in range(max(lo - 1, 0), hi - 1)]
        return parts[0] if len(parts) == 1 else jnp.concatenate(parts, axis=0)

    def product(rows_of, columns_of):
        acc = None
        for i in range(blocks * blk // cut):
            columns = slice(i * cut, (i + 1) * cut)
            d = lax.dot_general(
                strips(*rows_of, columns), strips(*columns_of, columns), NT,
                preferred_element_type=jnp.float32,
            )
            acc = d if acc is None else acc + d
        return acc

    def open_gram(which):
        if which == 0:
            gram0[0] = jnp.zeros(gram0.shape[1:], jnp.float32)
            gram0[0, :, 0 : (S - 1) * panel] = product((0, S - 1), (0, S - 1))
        elif which == 1:
            gram1[0] = product((S - 1, S), (0, S))
        else:
            gram2[0, 0:panel] = product((S, S + 1), (0, S))
            gram2[0, panel : 2 * panel, :] = jnp.zeros((panel, S * panel), jnp.float32)
            gram2[0, panel : 2 * panel, 0:panel] = product((S, S + 1), (S, S + 1))
        gram_copy(which, 0).start()

    def join(which, stage):
        src, dst = grams[which]
        gram_copy(which, stage).wait_recv()
        src[stage + 1] = src[stage] + dst[stage]
        if stage + 1 < stages:
            gram_copy(which, stage + 1).start()

    joined = [0, 0, 0]

    def more(which):
        if joined[which] < stages:
            join(which, joined[which])
            joined[which] += 1

    for k in range(S):
        advance(k, 0)
        if k == S - 1:
            more(0)
        collect(k, 0)
        advance(k, 1)
        if k == S - 1:
            open_gram(1)
        relay(k, 0)
        collect(k, 1)
        if k == S - 2:
            open_gram(0)
        relay(k, 1)
        if k == S - 2:
            more(0)
        if k == S - 1:
            more(1)
            more(0)
    for h in range(HALVES):
        for j in range(CHUNKS):
            finish(S - 1, h, j)
        if h == 0:
            more(1)
    open_gram(2)
    for stage in range(stages):
        for which in range(3):
            more(which)

    scale = 1.0 / (n * blocks * blk)
    w = S * panel
    for which, at in ((1, S - 1), (2, S)):
        side = grams[which][0][stages, 0:panel, 0 : at * panel] * scale
        gram_ref[0, at * panel : (at + 1) * panel, 0 : at * panel] = side
        gram_ref[0, 0 : at * panel, at * panel : (at + 1) * panel] = side.T
    v = (S - 1) * panel
    gram_ref[0, 0:v, 0:v] = gram0[stages, :, 0:v] * scale
    gram_ref[0, v:w, v:w] = gram1[stages, :, v:w] * scale
    gram_ref[0, w : w + panel, w : w + panel] = gram2[stages, panel : 2 * panel, 0:panel] * scale

    for k in range(S):
        for h in range(HALVES):
            for j in range(CHUNKS):
                near_copy(k, h, j).wait_send()

                @pl.when(sends_far)
                def _():
                    far_copy(k, h, j).wait_send()

    for which in range(3):
        for stage in range(stages):
            gram_copy(which, stage).wait_send()


def body(n, start, tiles, cols, counts):
    panel, rows_dev = start.shape
    blocks, slots, blk, _ = tiles.shape
    total = blocks * slots
    rows = panel // HALVES
    stages = n.bit_length() - 1
    code = schedule(cols, counts, n)
    w = S * panel
    vmem = pl.BlockSpec(memory_space=pltpu.VMEM)
    travel = pltpu.VMEM((S, HALVES, blocks, rows, blk), jnp.float32)
    dma = pltpu.SemaphoreType.DMA
    return pl.pallas_call(
        functools.partial(kernel, n, blocks, slots),
        out_shape=(
            jax.ShapeDtypeStruct((S, panel, rows_dev), jnp.bfloat16),
            jax.ShapeDtypeStruct((1, w + panel, w + panel), jnp.float32),
        ),
        in_specs=[vmem, vmem, pl.BlockSpec(memory_space=pltpu.SMEM)],
        out_specs=(vmem, vmem),
        scratch_shapes=[
            pltpu.VMEM((total, rows, blk), jnp.float32),
            pltpu.VMEM((total + 1, rows, blk), jnp.float32),
            pltpu.VMEM((total + 1, rows, blk), jnp.float32),
            travel, travel, travel, travel,
            pltpu.VMEM((stages + 1, w - panel, w), jnp.float32),
            pltpu.VMEM((stages, w - panel, w), jnp.float32),
            pltpu.VMEM((stages + 1, panel, w), jnp.float32),
            pltpu.VMEM((stages, panel, w), jnp.float32),
            pltpu.VMEM((stages + 1, 2 * panel, w), jnp.float32),
            pltpu.VMEM((stages, 2 * panel, w), jnp.float32),
            dma((S, HALVES, CHUNKS)),
            dma((S, HALVES, CHUNKS)),
            dma((S, HALVES, CHUNKS)),
            dma((S, HALVES, CHUNKS)),
            dma((3, stages)),
            dma((3, stages)),
        ],
        compiler_params=pltpu.CompilerParams(
            collective_id=0, has_side_effects=True, vmem_limit_bytes=40 * 1024 * 1024
        ),
    )(start, tiles.reshape(total, blk, blk), code)


def solution(mesh):
    return jax.shard_map(
        functools.partial(body, mesh.shape["rows"]),
        mesh=mesh,
        in_specs=(P("rhs", "rows"), P("rows", None, None, None), P("rows", None), P("rows")),
        out_specs=(P(None, "rhs", "rows"), P("rhs", None, None)),
        check_vma=False,
    )
```

```python
import functools

import jax
import jax.numpy as jnp
from jax import lax
from jax.experimental import pallas as pl
from jax.experimental.pallas import tpu as pltpu
from jax.sharding import PartitionSpec as P

S = 4
HALVES = 2
CHUNKS = 4
UNROLL = 16
MESH = pl.DeviceIdType.MESH


def schedule(cols, counts, devices):
    blocks, slots = cols.shape
    total = blocks * slots
    r = lax.axis_index("rows")
    rel = cols - (r - 1) * blocks
    side = rel // blocks
    even = r % 2 == 0
    group = jnp.where(side == 1, 2, jnp.where((side == 0) == even, 0, 1))
    target = group * blocks + rel % blocks
    used = jnp.arange(slots, dtype=jnp.int32)[None, :] < counts[:, None]
    target = jnp.where(used, target, 3 * blocks).reshape(-1)
    item = jnp.arange(total, dtype=jnp.int32)
    earlier = target[None, :] < target[:, None]
    tied = (target[None, :] == target[:, None]) & (item[None, :] < item[:, None])
    rank = jnp.sum(earlier | tied, axis=1, dtype=jnp.int32)
    opens = jnp.logical_not(jnp.any(tied, axis=1)).astype(jnp.int32)
    code = item * 2 + opens
    placed = jnp.sum(jnp.where(rank[None, :] == item[:, None], code[None, :], 0), axis=1, dtype=jnp.int32)
    c = jnp.arange(3 * blocks, dtype=jnp.int32)[:, None]
    upto = jnp.sum(target[None, :] <= c, axis=1, dtype=jnp.int32)
    here = jnp.any(target[None, :] == c, axis=1)
    last = jnp.where(here, upto - 1, total)
    return jnp.concatenate([placed, last])


def kernel(
    n, blocks, slots, start_ref, tiles_hbm, code_ref, basis_ref, gram_ref,
    tiles, products, sums0, sums1, far_out, far_in, near_out, near_in,
    gram0, gram0_in, gram1, gram1_in, gram2, gram2_in,
    tile_sem, far_send, far_recv, near_send, near_recv, gram_send, gram_recv,
):
    total = blocks * slots
    sums = (sums0, sums1)
    grams = ((gram0, gram0_in), (gram1, gram1_in), (gram2, gram2_in))
    rows = start_ref.shape[0] // HALVES
    blk = tiles.shape[-1]
    per = blocks // CHUNKS
    stages = n.bit_length() - 1
    r = lax.axis_index("rows")
    parity = r % 2
    step = 4 * parity - 2
    to, frm = r + step, r - step
    sends_far = jnp.logical_and(to >= 0, to < n)
    takes_far = jnp.logical_and(frm >= 0, frm < n)
    to = jnp.clip(to, 0, n - 1)
    frm = jnp.clip(frm, 0, n - 1)
    partner = r + 1 - 2 * parity

    def across(stage):
        width = 1 << stage
        return r + width - 2 * width * ((r // width) % 2)

    def load(j):
        part = pl.ds(j * per * slots, per * slots)
        return pltpu.make_async_copy(tiles_hbm.at[part], tiles.at[part], tile_sem.at[j])

    for j in range(CHUNKS):
        load(j).start()

    barrier = pltpu.get_barrier_semaphore()
    for stage in range(stages):
        pl.semaphore_signal(barrier, inc=1, device_id={"rows": across(stage)}, device_id_type=MESH)

    @pl.when(sends_far)
    def _():
        pl.semaphore_signal(barrier, inc=1, device_id={"rows": to}, device_id_type=MESH)

    @pl.when(takes_far)
    def _():
        pl.semaphore_signal(barrier, inc=1, device_id={"rows": frm}, device_id_type=MESH)

    for h in range(HALVES):
        sums[h][total] = jnp.zeros((rows, blk), jnp.float32)
    pl.semaphore_wait(barrier, stages + sends_far.astype(jnp.int32) + takes_far.astype(jnp.int32))

    def far_copy(k, h, j):
        part = pl.ds(j * per, per)
        return pltpu.make_async_remote_copy(
            src_ref=far_out.at[k, h, part], dst_ref=far_in.at[k, h, part],
            send_sem=far_send.at[k, h, j], recv_sem=far_recv.at[k, h, j],
            device_id={"rows": to}, device_id_type=MESH,
        )

    def near_copy(k, h, j):
        part = pl.ds(j * per, per)
        return pltpu.make_async_remote_copy(
            src_ref=near_out.at[k, h, part], dst_ref=near_in.at[k, h, part],
            send_sem=near_send.at[k, h, j], recv_sem=near_recv.at[k, h, j],
            device_id={"rows": partner}, device_id_type=MESH,
        )

    def gram_copy(which, stage):
        src, dst = grams[which]
        return pltpu.make_async_remote_copy(
            src_ref=src.at[stage], dst_ref=dst.at[stage],
            send_sem=gram_send.at[which, stage], recv_sem=gram_recv.at[which, stage],
            device_id={"rows": across(stage)}, device_id_type=MESH,
        )

    zero = jnp.zeros((rows, blk), jnp.bfloat16)

    def multiply(pair, upper, lower):
        a, b = 2 * pair * slots, (2 * pair + 1) * slots
        left = jnp.concatenate(
            [jnp.concatenate([upper, zero], axis=1), jnp.concatenate([zero, lower], axis=1)], axis=0
        )
        for t in range(0, slots, 2):
            right = jnp.concatenate(
                [
                    jnp.concatenate([tiles[a + t], tiles[a + t + 1]], axis=1),
                    jnp.concatenate([tiles[b + t], tiles[b + t + 1]], axis=1),
                ],
                axis=0,
            )
            out = jnp.dot(left, right, preferred_element_type=jnp.float32)
            products[a + t] = out[:rows, :blk]
            products[a + t + 1] = out[:rows, blk:]
            products[b + t] = out[rows:, :blk]
            products[b + t + 1] = out[rows:, blk:]

    def advance(k, h, j):
        if k > 0:
            values = finish(k - 1, h, j)
        else:
            if h == 0:
                load(j).wait()
            values = [
                start_ref[h * rows : (h + 1) * rows, c * blk : (c + 1) * blk]
                for c in range(j * per, (j + 1) * per)
            ]
        for p in range(per // 2):
            multiply(j * per // 2 + p, values[2 * p], values[2 * p + 1])

    def collect(k, h):
        place = sums[h]

        def some(i, acc):
            for u in range(UNROLL):
                s = i * UNROLL + u
                code = code_ref[s]
                acc = jnp.where((code & 1) == 1, 0.0, acc) + products[code >> 1]
                place[s] = acc
            return acc

        lax.fori_loop(0, total // UNROLL, some, jnp.zeros((rows, blk), jnp.float32))
        for j in range(CHUNKS):
            for c in range(j * per, (j + 1) * per):
                far_out[k, h, c] = place[code_ref[total + c]]

            @pl.when(sends_far)
            def _():
                far_copy(k, h, j).start()

    def relay(k, h, j):
        place = sums[h]
        for c in range(j * per, (j + 1) * per):
            near_out[k, h, c] = place[code_ref[total + blocks + c]]

        @pl.when(takes_far)
        def _():
            far_copy(k, h, j).wait_recv()
            part = pl.ds(j * per, per)
            near_out[k, h, part] += far_in[k, h, part]

        near_copy(k, h, j).start()

    def finish(k, h, j):
        place = sums[h]
        near_copy(k, h, j).wait_recv()
        values = []
        for c in range(j * per, (j + 1) * per):
            value = (place[code_ref[total + 2 * blocks + c]] + near_in[k, h, c]).astype(jnp.bfloat16)
            basis_ref[k, h * rows : (h + 1) * rows, c * blk : (c + 1) * blk] = value
            values.append(value)
        return values

    NT = (((1,), (1,)), ((), ()))
    panel = HALVES * rows
    cut = 2 * blk

    def strips(lo, hi, columns):
        parts = [start_ref[:, columns]] if lo == 0 else []
        parts += [basis_ref[k, :, columns] for k in range(max(lo - 1, 0), hi - 1)]
        return parts[0] if len(parts) == 1 else jnp.concatenate(parts, axis=0)

    def product(rows_of, columns_of):
        acc = None
        for i in range(blocks * blk // cut):
            columns = slice(i * cut, (i + 1) * cut)
            d = lax.dot_general(
                strips(*rows_of, columns), strips(*columns_of, columns), NT,
                preferred_element_type=jnp.float32,
            )
            acc = d if acc is None else acc + d
        return acc

    def triangle(at, to):
        place = at * (at + 1) // 2 + to
        return place // S * panel, place % S * panel

    def open_gram(which):
        if which == 0:
            g = product((0, S - 1), (0, S - 1))
            gram0[0] = jnp.zeros(gram0.shape[1:], jnp.float32)
            for at in range(S - 1):
                for to in range(at + 1):
                    row, lane = triangle(at, to)
                    gram0[0, row : row + panel, lane : lane + panel] = g[
                        at * panel : (at + 1) * panel, to * panel : (to + 1) * panel
                    ]
        elif which == 1:
            gram1[0] = product((S - 1, S), (0, S))
        else:
            gram2[0, 0:panel] = product((S, S + 1), (0, S))
            own = product((S, S + 1), (S, S + 1))
            gram2[0, panel : panel + panel // S] = jnp.concatenate(
                [own[q * panel // S : (q + 1) * panel // S] for q in range(S)], axis=1
            )
        gram_copy(which, 0).start()

    def join(which, stage):
        src, dst = grams[which]
        gram_copy(which, stage).wait_recv()
        src[stage + 1] = src[stage] + dst[stage]
        if stage + 1 < stages:
            gram_copy(which, stage + 1).start()

    joined = [0, 0, 0]

    def more(which):
        if joined[which] < stages:
            join(which, joined[which])
            joined[which] += 1

    for k in range(S):
        for j in range(CHUNKS):
            advance(k, 0, j)
            if k > 0:
                relay(k - 1, 1, j)
        collect(k, 0)
        if k == S - 1:
            more(0)
        for j in range(CHUNKS):
            advance(k, 1, j)
        relay(k, 0, 0)
        collect(k, 1)
        for j in range(1, CHUNKS):
            relay(k, 0, j)
        if k >= S - 2:
            open_gram(k - (S - 2))
        if k == S - 1:
            more(0)
    for j in range(CHUNKS):
        finish(S - 1, 0, j)
        relay(S - 1, 1, j)
    more(1)
    more(0)
    for j in range(CHUNKS):
        finish(S - 1, 1, j)
    more(1)
    open_gram(2)
    for stage in range(stages):
        for which in range(3):
            more(which)

    scale = 1.0 / (n * blocks * blk)
    w = S * panel
    for which, at in ((1, S - 1), (2, S)):
        side = grams[which][0][stages, 0:panel, 0 : at * panel] * scale
        gram_ref[0, at * panel : (at + 1) * panel, 0 : at * panel] = side
        gram_ref[0, 0 : at * panel, at * panel : (at + 1) * panel] = side.T
    v = (S - 1) * panel
    for at in range(S - 1):
        for to in range(at + 1):
            row, lane = triangle(at, to)
            block = gram0[stages, row : row + panel, lane : lane + panel] * scale
            gram_ref[0, at * panel : (at + 1) * panel, to * panel : (to + 1) * panel] = block
            if to < at:
                gram_ref[0, to * panel : (to + 1) * panel, at * panel : (at + 1) * panel] = block.T
    gram_ref[0, v:w, v:w] = gram1[stages, :, v:w] * scale
    for q in range(S):
        gram_ref[0, w + q * panel // S : w + (q + 1) * panel // S, w : w + panel] = (
            gram2[stages, panel : panel + panel // S, q * panel : (q + 1) * panel] * scale
        )

    for k in range(S):
        for h in range(HALVES):
            for j in range(CHUNKS):
                near_copy(k, h, j).wait_send()

                @pl.when(sends_far)
                def _():
                    far_copy(k, h, j).wait_send()

    for which in range(3):
        for stage in range(stages):
            gram_copy(which, stage).wait_send()


def body(n, start, tiles, cols, counts):
    panel, rows_dev = start.shape
    blocks, slots, blk, _ = tiles.shape
    total = blocks * slots
    rows = panel // HALVES
    stages = n.bit_length() - 1
    code = schedule(cols, counts, n)
    w = S * panel
    first = -(-(S * (S - 1) // 2) // S)
    vmem = pl.BlockSpec(memory_space=pltpu.VMEM)
    travel = pltpu.VMEM((S, HALVES, blocks, rows, blk), jnp.float32)
    dma = pltpu.SemaphoreType.DMA
    return pl.pallas_call(
        functools.partial(kernel, n, blocks, slots),
        out_shape=(
            jax.ShapeDtypeStruct((S, panel, rows_dev), jnp.bfloat16),
            jax.ShapeDtypeStruct((1, w + panel, w + panel), jnp.float32),
        ),
        in_specs=[vmem, pl.BlockSpec(memory_space=pl.ANY), pl.BlockSpec(memory_space=pltpu.SMEM)],
        out_specs=(vmem, vmem),
        scratch_shapes=[
            pltpu.VMEM((total, blk, blk), jnp.bfloat16),
            pltpu.VMEM((total, rows, blk), jnp.float32),
            pltpu.VMEM((total + 1, rows, blk), jnp.float32),
            pltpu.VMEM((total + 1, rows, blk), jnp.float32),
            travel, travel, travel, travel,
            pltpu.VMEM((stages + 1, first * panel, w), jnp.float32),
            pltpu.VMEM((stages, first * panel, w), jnp.float32),
            pltpu.VMEM((stages + 1, panel, w), jnp.float32),
            pltpu.VMEM((stages, panel, w), jnp.float32),
            pltpu.VMEM((stages + 1, panel + panel // S, w), jnp.float32),
            pltpu.VMEM((stages, panel + panel // S, w), jnp.float32),
            dma((CHUNKS,)),
            dma((S, HALVES, CHUNKS)),
            dma((S, HALVES, CHUNKS)),
            dma((S, HALVES, CHUNKS)),
            dma((S, HALVES, CHUNKS)),
            dma((3, stages)),
            dma((3, stages)),
        ],
        compiler_params=pltpu.CompilerParams(
            collective_id=0, has_side_effects=True, vmem_limit_bytes=60 * 1024 * 1024
        ),
    )(start, tiles.reshape(total, blk, blk), code)


def solution(mesh):
    return jax.shard_map(
        functools.partial(body, mesh.shape["rows"]),
        mesh=mesh,
        in_specs=(P("rhs", "rows"), P("rows", None, None, None), P("rows", None), P("rows")),
        out_specs=(P(None, "rhs", "rows"), P("rhs", None, None)),
        check_vma=False,
    )
```
